512 devices in a mesh: blk: 32 (over z, core), grp: 16 (over y, x).
Axes of the slice: x: 4, y: 4, z: 16, core: 2. Of those that a mesh axis runs over, the one named last changes fastest.
Arguments:
- labels: float32 [16, 16384, 256], P('grp', 'blk'), may hold values from 0.1 to 10
- tiles: bfloat16 [16, 128, 16, 128, 128], P('grp', 'blk'), may hold values from 0.001 to 1
- tile_cols: int32 [16, 128, 16], P('grp', 'blk'), may hold values from 0 to 23
- tile_count: int32 [16, 128], P('grp', 'blk'), may hold values from 4 to 16
- send_blocks: int32 [16, 32, 16, 1], P('grp', 'blk'), may hold values from 0 to 3
Outputs:
- spread: float32 [16, 16384, 256], P('grp', 'blk')
The draws below stay inside these ranges and needn't reach their ends.
All inputs are finite; a program needn't handle non-finite values.
Results may differ from the reference program's by a relative error of at most 0.0006.
Values may be sent and summed in bfloat16 or wider, within the bound.
A program may use at most 64 MiB of HBM per device.

```python
import math
import jax
import jax.numpy as jnp
from jax import lax

C = 256
BS = 128
RB = 4
KMAX = 16
HB = 2
BMAX = 1
ITERS = 3
NE = 24
NR = 16384
N_BLK = 32
N_GRP = 16


def log_between(uniform_draw, lower, upper):
    return jnp.exp(math.log(lower) + uniform_draw * (math.log(upper) - math.log(lower)))


def draw_labels(key, part):
    key = jax.random.fold_in(key, 11)
    key_class, key_peak, key_base = jax.random.split(key, 3)
    dominant = jax.random.randint(key_class, (N_GRP, NR, 1), 0, C)
    is_peak = jnp.arange(C, dtype=jnp.int32)[None, None, :] == dominant
    peak_value = log_between(jax.random.uniform(key_peak, (N_GRP, NR, 1), jnp.float32), 3.0, 10.0)
    background = log_between(jax.random.uniform(key_base, (N_GRP, NR, C), jnp.float32), 0.1, 0.4)
    return jnp.where(is_peak, peak_value, background).astype(jnp.float32)


def edge_weights(uniform_draw, share, strong_low, weak_high):
    strong = log_between(jnp.clip(uniform_draw / share, 0.0, 1.0), strong_low, 1.0)
    weak = log_between(jnp.clip((uniform_draw - share) / (1.0 - share), 0.0, 1.0), 0.001, weak_high)
    return jnp.where(uniform_draw < share, strong, weak)


def draw_tiles(key, part):
    key = jax.random.fold_in(key, 23)
    uniform_draw = jax.random.uniform(key, (N_GRP, N_BLK * RB, KMAX, BS, BS), jnp.float32)
    weights = edge_weights(uniform_draw, 0.0625, 0.1, 0.01)
    return weights.astype(jnp.bfloat16)


def with_ends(drawn, own_key, least, largest):
    longest = drawn.shape.index(max(drawn.shape))
    spots = []
    for shift in (0, 1):
        where = [jax.random.randint(jax.random.fold_in(own_key, axis), (), 0, length) for axis, length in enumerate(drawn.shape)]
        where[longest] = (where[longest] + shift) % drawn.shape[longest]
        spots.append(tuple(where))
    return drawn.at[spots[0]].set(least).at[spots[1]].set(largest)


def setup_inputs(seed: int = 0) -> dict:
    splits = jax.random.split(jax.random.key(seed), 6)
    return {
        "labels": draw_labels(jax.random.fold_in(splits[5], 71), 0),
        "tiles": draw_tiles(jax.random.fold_in(splits[5], 71), 0),
        "tile_cols": with_ends(jax.random.randint(splits[2], (N_GRP, N_BLK * RB, KMAX), 0, NE), jax.random.fold_in(splits[2], 1), 0, NE - 1).astype(jnp.int32),
        "tile_count": with_ends(jax.random.randint(splits[3], (N_GRP, N_BLK * RB), 4, KMAX + 1), jax.random.fold_in(splits[3], 1), 4, KMAX).astype(jnp.int32),
        "send_blocks": with_ends(jax.random.randint(splits[4], (N_GRP, N_BLK, N_GRP, BMAX), 0, RB), jax.random.fold_in(splits[4], 1), 0, RB - 1).astype(jnp.int32),
    }


def reference(labels, tiles, tile_cols, tile_count, send_blocks):
    n_dev = N_GRP * N_BLK
    slots = jnp.arange(KMAX, dtype=jnp.int32)
    valid = slots[None, None, :] < tile_count[:, :, None]
    row_sums = lax.optimization_barrier(jnp.sum(tiles, axis=-1, dtype=jnp.float32))
    deg = lax.optimization_barrier(jnp.sum(jnp.where(valid[..., None], row_sums, 0.0), axis=2))
    scale = lax.rsqrt(deg).reshape(N_GRP, NR)
    tiles_dev = tiles.reshape(n_dev, RB, KMAX, BS, BS)
    cols_dev = tile_cols.reshape(n_dev, RB, KMAX)
    valid_dev = valid.reshape(n_dev, RB, KMAX)
    dev_ids = jnp.arange(n_dev, dtype=jnp.int32)
    band_ids = jnp.arange(N_GRP, dtype=jnp.int32)
    field = labels
    for step in range(ITERS):
        scaled = (scale[..., None] * field).astype(jnp.bfloat16)
        padded = jnp.pad(scaled, ((0, 0), (HB * BS, HB * BS), (0, 0)))
        scaled_blocks = scaled.reshape(N_GRP, N_BLK * RB, BS, C)

        def dev_step(inputs):
            dev, tile_d, col_d, valid_d = inputs
            band = dev // N_BLK
            place = dev % N_BLK
            start = (place * (RB * BS)).astype(jnp.int32)
            local = lax.dynamic_slice(padded, (band, start, jnp.int32(0)), (1, (RB + 2 * HB) * BS, C))
            local = local.reshape(RB + 2 * HB, BS, C)
            picks = send_blocks[:, place, band, :]
            cross = scaled_blocks[band_ids[:, None], place * RB + picks]
            ext = jnp.concatenate([local, cross.reshape(N_GRP * BMAX, BS, C)], axis=0)
            chosen = jnp.where(valid_d[..., None, None], ext[col_d], jnp.zeros((), jnp.bfloat16))
            return jnp.einsum('rkij,rkjc->ric', tile_d.astype(jnp.float32), chosen.astype(jnp.float32))
        summed = lax.map(dev_step, (dev_ids, tiles_dev, cols_dev, valid_dev))
        summed = summed.reshape(N_GRP, NR, C)
        update = 0.9 * scale[..., None] * summed + 0.1 * labels
        field = update / lax.optimization_barrier(jnp.mean(update, axis=-1, keepdims=True))
    return field
```

```python
import functools

import jax
import jax.numpy as jnp
from jax import lax
from jax.experimental import pallas as pl
from jax.experimental.pallas import tpu as pltpu
from jax.sharding import PartitionSpec as P

HB = 2
ITERS = 3
HALVES = 2
MESH = pl.DeviceIdType.MESH


def kernel(n_grp, n_blk, cols_ref, count_ref, pick_ref, labels_hbm, tiles_hbm, out_ref, *scratch):
    ext = scratch[0:6]
    own = scratch[6:12]
    staged = scratch[12:18]
    ext_sum = scratch[18:20]
    own_sum = scratch[20:22]
    staged_sum = scratch[22:24]
    (tiles, labels, scale, anchor_sum, coef_h, coef_l, col, load_sem, send_sem, recv_sem,
     send_sum, recv_sum) = scratch[24:]
    n_rows, kmax, bsize = tiles.shape[0], tiles.shape[1], tiles.shape[2]
    classes = labels.shape[2]
    half = classes // HALVES
    local = n_rows + 2 * HB
    zero = local + n_grp
    me = lax.axis_index("grp")
    place = lax.axis_index("blk")
    after = lax.rem(place + 1, n_blk)
    before = lax.rem(place + n_blk - 1, n_blk)

    def load(r):
        return (
            pltpu.make_async_copy(tiles_hbm.at[0, r], tiles.at[r], load_sem.at[r]),
            pltpu.make_async_copy(labels_hbm.at[0, pl.ds(r * bsize, bsize)], labels.at[r], load_sem.at[n_rows + r]),
        )

    for r in range(n_rows):
        for copy in load(r):
            copy.start()

    barrier = pltpu.get_barrier_semaphore()

    def greet(p, carry):
        pl.semaphore_signal(barrier, inc=1, device_id={"grp": lax.rem(me + p, n_grp)}, device_id_type=MESH)
        return carry

    lax.fori_loop(1, n_grp, greet, 0)
    pl.semaphore_signal(barrier, inc=1, device_id={"blk": after}, device_id_type=MESH)
    pl.semaphore_signal(barrier, inc=1, device_id={"blk": before}, device_id_type=MESH)

    def name_row(r, carry):
        used = count_ref[0, r]
        for k in range(kmax):
            c = cols_ref[0, r, k]
            block = place * n_rows + c - HB
            outside = (c < local) & ((block < 0) | (block >= n_blk * n_rows))
            col[r, k] = jnp.where((k < used) & jnp.logical_not(outside), c, zero)
        return carry

    lax.fori_loop(0, n_rows, name_row, 0)
    for ref in ext:
        ref[zero] = jnp.zeros((bsize, half), jnp.bfloat16)
    for ref in ext_sum:
        ref[zero] = jnp.zeros((1, bsize), jnp.float32)

    def keep(t, h, r, value):
        own[t * HALVES + h][r] = value
        ext[t * HALVES + h][HB + r] = value

    def keep_sum(t, r, total):
        at_row = lax.broadcasted_iota(jnp.int32, (bsize, bsize), 0)
        at_col = lax.broadcasted_iota(jnp.int32, (bsize, bsize), 1)
        spread = jnp.where(at_row == at_col, jnp.broadcast_to(total, (bsize, bsize)), 0.0)
        row = jnp.sum(spread, axis=0, keepdims=True)
        own_sum[t][r] = row
        ext_sum[t][HB + r] = row

    def halo_copies(mine, theirs, ssem, rsem, t):
        return (
            pltpu.make_async_remote_copy(
                src_ref=mine.at[pl.ds(n_rows - HB, HB)], dst_ref=theirs.at[pl.ds(0, HB)],
                send_sem=ssem.at[t, 1], recv_sem=rsem.at[t, 1], device_id={"blk": after}, device_id_type=MESH,
            ),
            pltpu.make_async_remote_copy(
                src_ref=mine.at[pl.ds(0, HB)], dst_ref=theirs.at[pl.ds(HB + n_rows, HB)],
                send_sem=ssem.at[t, 2], recv_sem=rsem.at[t, 2], device_id={"blk": before}, device_id_type=MESH,
            ),
        )

    def send(mine, out, theirs, ssem, rsem, t):
        def one(p, carry):
            other = lax.rem(me + p, n_grp)
            out[p] = mine[pick_ref[0, 0, other]]
            pltpu.make_async_remote_copy(
                src_ref=out.at[p], dst_ref=theirs.at[local + me],
                send_sem=ssem.at[t, 0], recv_sem=rsem.at[t, 0], device_id={"grp": other}, device_id_type=MESH,
            ).start()
            return carry

        lax.fori_loop(1, n_grp, one, 0)
        for copy in halo_copies(mine, theirs, ssem, rsem, t):
            copy.start()
        theirs[local + me] = mine[pick_ref[0, 0, me]]

    def wait_sent(mine, out, theirs, ssem, rsem, t):
        whole = out.at[pl.ds(1, n_grp - 1)]
        pltpu.make_async_copy(whole, whole, ssem.at[t, 0]).wait()
        for copy in halo_copies(mine, theirs, ssem, rsem, t):
            copy.wait_send()

    def wait_here(mine, theirs, ssem, rsem, t):
        whole = theirs.at[pl.ds(local, n_grp - 1)]
        pltpu.make_async_copy(whole, whole, rsem.at[t, 0]).wait()
        for copy in halo_copies(mine, theirs, ssem, rsem, t):
            copy.wait_recv()

    def field(t, h):
        i = t * HALVES + h
        return own[i], staged[i], ext[i], send_sem, recv_sem, i

    def sums(t):
        return own_sum[t], staged_sum[t], ext_sum[t], send_sum, recv_sum, t

    def arrived(of):
        wait_here(of[0], of[2], *of[3:])

    def product(t, h, r):
        blocks = ext[t * HALVES + h]
        lhs = jnp.concatenate([tiles[r, k] for k in range(kmax)], axis=1)
        rhs = jnp.concatenate([blocks[col[r, k]] for k in range(kmax)], axis=0)
        return jnp.dot(lhs, rhs, preferred_element_type=jnp.float32)

    for r in range(n_rows):
        for copy in load(r):
            copy.wait()

    def start_row(r, carry):
        total = jnp.zeros((bsize, bsize), jnp.float32)
        used = count_ref[0, r]
        for k in range(kmax):
            total += tiles[r, k].astype(jnp.float32) * jnp.where(k < used, 1.0, 0.0)
        deg = jnp.sum(total, axis=1, keepdims=True)
        factor = jnp.broadcast_to(lax.rsqrt(deg), (bsize, half))
        scale[r] = factor
        values = []
        for h in range(HALVES):
            value = (factor * labels[r, :, h * half:(h + 1) * half]).astype(jnp.bfloat16)
            keep(0, h, r, value)
            values.append(value.astype(jnp.float32))
        keep_sum(0, r, jnp.sum(values[0] + values[1], axis=1, keepdims=True))
        return carry

    lax.fori_loop(0, n_rows, start_row, 0)
    pl.semaphore_wait(barrier, n_grp + 1)
    send(*field(0, 0))
    send(*sums(0))
    send(*field(0, 1))

    def anchor_row(r, carry):
        total = jnp.sum(labels[r, :, :half] + labels[r, :, half:], axis=1, keepdims=True)
        anchor_sum[r] = jnp.broadcast_to(total, (bsize, half))
        return carry

    lax.fori_loop(0, n_rows, anchor_row, 0)

    for t in range(ITERS - 1):
        arrived(sums(t))
        arrived(field(t, 0))

        def first_row(r, carry, t=t):
            h_first = product(t, 0, r)
            total = jnp.zeros((bsize, bsize), jnp.float32)
            for k in range(kmax):
                total += tiles[r, k].astype(jnp.float32) * ext_sum[t][col[r, k]]
            total = jnp.broadcast_to(jnp.sum(total, axis=1, keepdims=True), (bsize, half))
            factor = scale[r]
            mean = (0.9 * factor * total + 0.1 * anchor_sum[r]) * (1.0 / classes)
            inverse = factor / mean
            for_h = 0.9 * factor * inverse
            for_l = 0.1 * inverse
            coef_h[r] = for_h
            coef_l[r] = for_l
            value = for_h * h_first + for_l * labels[r, :, :half]
            keep(t + 1, 0, r, value.astype(jnp.bfloat16))
            return carry

        lax.fori_loop(0, n_rows, first_row, 0)
        send(*field(t + 1, 0))
        arrived(field(t, 1))

        def second_row(r, carry, t=t):
            value = coef_h[r] * product(t, 1, r) + coef_l[r] * labels[r, :, half:]
            value = value.astype(jnp.bfloat16)
            keep(t + 1, 1, r, value)
            if t + 1 < ITERS - 1:
                both = value.astype(jnp.float32) + own[(t + 1) * HALVES][r].astype(jnp.float32)
                keep_sum(t + 1, r, jnp.sum(both, axis=1, keepdims=True))
            return carry

        lax.fori_loop(0, n_rows, second_row, 0)
        if t + 1 < ITERS - 1:
            send(*sums(t + 1))
        send(*field(t + 1, 1))

    last = ITERS - 1

    def update(h, r):
        return 0.9 * scale[r] * product(last, h, r) + 0.1 * labels[r, :, h * half:(h + 1) * half]

    arrived(field(last, 0))

    def last_first(r, carry):
        coef_h[r] = update(0, r)
        return carry

    lax.fori_loop(0, n_rows, last_first, 0)
    arrived(field(last, 1))

    def last_second(r, carry):
        second = update(1, r)
        first = coef_h[r]
        mean = jnp.sum(first + second, axis=1, keepdims=True) * (1.0 / classes)
        inverse = jnp.broadcast_to(1.0 / mean, (bsize, half))
        rows = pl.ds(pl.multiple_of(r * bsize, bsize), bsize)
        out_ref[0, rows, :half] = first * inverse
        out_ref[0, rows, half:] = second * inverse
        return carry

    lax.fori_loop(0, n_rows, last_second, 0)
    for t in range(ITERS):
        if t < ITERS - 1:
            wait_sent(*sums(t))
        for h in range(HALVES):
            wait_sent(*field(t, h))


def solution(mesh):
    n_grp, n_blk = mesh.shape["grp"], mesh.shape["blk"]

    def on_device(labels, tiles, tile_cols, tile_count, send_blocks):
        n_rows, kmax, bsize = tiles.shape[1:4]
        classes = labels.shape[2]
        half = classes // HALVES
        names = n_rows + 2 * HB + n_grp + 1
        count = ITERS * HALVES
        smem = pl.BlockSpec(memory_space=pltpu.SMEM)
        whole = pltpu.VMEM((n_rows, bsize, half), jnp.float32)
        return pl.pallas_call(
            functools.partial(kernel, n_grp, n_blk),
            name="spreading",
            out_shape=jax.ShapeDtypeStruct(labels.shape, jnp.float32),
            in_specs=[smem] * 3 + [pl.BlockSpec(memory_space=pl.ANY)] * 2,
            out_specs=pl.BlockSpec(memory_space=pltpu.VMEM),
            scratch_shapes=[pltpu.VMEM((names, bsize, half), jnp.bfloat16)] * count
            + [pltpu.VMEM((n_rows, bsize, half), jnp.bfloat16)] * count
            + [pltpu.VMEM((n_grp, bsize, half), jnp.bfloat16)] * count
            + [pltpu.VMEM((names, 1, bsize), jnp.float32)] * (ITERS - 1)
            + [pltpu.VMEM((n_rows, 1, bsize), jnp.float32)] * (ITERS - 1)
            + [pltpu.VMEM((n_grp, 1, bsize), jnp.float32)] * (ITERS - 1)
            + [
                pltpu.VMEM((n_rows, kmax, bsize, bsize), jnp.bfloat16),
                pltpu.VMEM((n_rows, bsize, classes), jnp.float32),
                whole,
                whole,
                whole,
                whole,
                pltpu.SMEM((n_rows, kmax), jnp.int32),
                pltpu.SemaphoreType.DMA((2 * n_rows,)),
                pltpu.SemaphoreType.DMA((count, 3)),
                pltpu.SemaphoreType.DMA((count, 3)),
                pltpu.SemaphoreType.DMA((ITERS - 1, 3)),
                pltpu.SemaphoreType.DMA((ITERS - 1, 3)),
            ],
            compiler_params=pltpu.CompilerParams(
                collective_id=0, has_side_effects=True, vmem_limit_bytes=60 << 20
            ),
        )(tile_cols, tile_count, send_blocks.reshape(1, 1, n_grp), labels, tiles)

    return jax.shard_map(
        on_device,
        mesh=mesh,
        in_specs=(
            P("grp", "blk", None),
            P("grp", "blk", None, None, None),
            P("grp", "blk", None),
            P("grp", "blk"),
            P("grp", "blk", None, None),
        ),
        out_specs=P("grp", "blk", None),
        check_vma=False,
    )
```

```python
import functools

import jax
import jax.numpy as jnp
from jax import lax
from jax.experimental import pallas as pl
from jax.experimental.pallas import tpu as pltpu
from jax.sharding import PartitionSpec as P

HB = 2
ITERS = 3
HALVES = 2
MESH = pl.DeviceIdType.MESH


def kernel(n_grp, n_blk, cols_hbm, count_hbm, pick_hbm, labels_hbm, tiles_hbm, out_ref, *scratch):
    ext = scratch[0:6]
    own = scratch[6:12]
    staged = scratch[12:18]
    ext_sum = scratch[18:20]
    own_sum = scratch[20:22]
    staged_sum = scratch[22:24]
    (tiles, labels, scale, anchor_sum, coef_h, coef_l, cols_ref, count_ref, pick_ref, col, load_sem, small_sem, send_sem, recv_sem,
     send_sum, recv_sum) = scratch[24:]
    n_rows, kmax, bsize = tiles.shape[0], tiles.shape[1], tiles.shape[2]
    classes = labels.shape[2]
    half = classes // HALVES
    local = n_rows + 2 * HB
    zero = local + n_grp
    me = lax.axis_index("grp")
    place = lax.axis_index("blk")
    after = lax.rem(place + 1, n_blk)
    before = lax.rem(place + n_blk - 1, n_blk)

    def load(r):
        return (
            pltpu.make_async_copy(tiles_hbm.at[0, r], tiles.at[r], load_sem.at[r]),
            pltpu.make_async_copy(labels_hbm.at[0, pl.ds(r * bsize, bsize)], labels.at[r], load_sem.at[n_rows + r]),
        )

    small = [
        pltpu.make_async_copy(src, dst, small_sem.at[i])
        for i, (src, dst) in enumerate(((cols_hbm, cols_ref), (count_hbm, count_ref), (pick_hbm, pick_ref)))
    ]
    for copy in small:
        copy.start()
    for r in range(n_rows):
        for copy in load(r):
            copy.start()

    barrier = pltpu.get_barrier_semaphore()

    def greet(p, carry):
        pl.semaphore_signal(barrier, inc=1, device_id={"grp": lax.rem(me + p, n_grp)}, device_id_type=MESH)
        return carry

    lax.fori_loop(1, n_grp, greet, 0)
    pl.semaphore_signal(barrier, inc=1, device_id={"blk": after}, device_id_type=MESH)
    pl.semaphore_signal(barrier, inc=1, device_id={"blk": before}, device_id_type=MESH)

    def name_row(r, carry):
        used = count_ref[0, r]
        for k in range(kmax):
            c = cols_ref[0, r, k]
            block = place * n_rows + c - HB
            outside = (c < local) & ((block < 0) | (block >= n_blk * n_rows))
            col[r, k] = jnp.where((k < used) & jnp.logical_not(outside), c, zero)
        return carry

    for copy in small:
        copy.wait()
    lax.fori_loop(0, n_rows, name_row, 0)
    for ref in ext:
        ref[zero] = jnp.zeros((bsize, half), jnp.bfloat16)
    for ref in ext_sum:
        ref[zero] = jnp.zeros((1, bsize), jnp.float32)

    def keep(t, h, r, value):
        own[t * HALVES + h][r] = value
        ext[t * HALVES + h][HB + r] = value

    def keep_sum(t, r, total):
        at_row = lax.broadcasted_iota(jnp.int32, (bsize, bsize), 0)
        at_col = lax.broadcasted_iota(jnp.int32, (bsize, bsize), 1)
        spread = jnp.where(at_row == at_col, jnp.broadcast_to(total, (bsize, bsize)), 0.0)
        row = jnp.sum(spread, axis=0, keepdims=True)
        own_sum[t][r] = row
        ext_sum[t][HB + r] = row

    def halo_copies(mine, theirs, ssem, rsem, t):
        return (
            pltpu.make_async_remote_copy(
                src_ref=mine.at[pl.ds(n_rows - HB, HB)], dst_ref=theirs.at[pl.ds(0, HB)],
                send_sem=ssem.at[t, 1], recv_sem=rsem.at[t, 1], device_id={"blk": after}, device_id_type=MESH,
            ),
            pltpu.make_async_remote_copy(
                src_ref=mine.at[pl.ds(0, HB)], dst_ref=theirs.at[pl.ds(HB + n_rows, HB)],
                send_sem=ssem.at[t, 2], recv_sem=rsem.at[t, 2], device_id={"blk": before}, device_id_type=MESH,
            ),
        )

    def send(mine, out, theirs, ssem, rsem, t):
        def one(p, carry):
            other = lax.rem(me + p, n_grp)
            out[p] = mine[pick_ref[0, 0, other]]
            pltpu.make_async_remote_copy(
                src_ref=out.at[p], dst_ref=theirs.at[local + me],
                send_sem=ssem.at[t, 0], recv_sem=rsem.at[t, 0], device_id={"grp": other}, device_id_type=MESH,
            ).start()
            return carry

        lax.fori_loop(1, n_grp, one, 0)
        for copy in halo_copies(mine, theirs, ssem, rsem, t):
            copy.start()
        theirs[local + me] = mine[pick_ref[0, 0, me]]

    def wait_sent(mine, out, theirs, ssem, rsem, t):
        whole = out.at[pl.ds(1, n_grp - 1)]
        pltpu.make_async_copy(whole, whole, ssem.at[t, 0]).wait()
        for copy in halo_copies(mine, theirs, ssem, rsem, t):
            copy.wait_send()

    def wait_here(mine, theirs, ssem, rsem, t):
        whole = theirs.at[pl.ds(local, n_grp - 1)]
        pltpu.make_async_copy(whole, whole, rsem.at[t, 0]).wait()
        for copy in halo_copies(mine, theirs, ssem, rsem, t):
            copy.wait_recv()

    def field(t, h):
        i = t * HALVES + h
        return own[i], staged[i], ext[i], send_sem, recv_sem, i

    def sums(t):
        return own_sum[t], staged_sum[t], ext_sum[t], send_sum, recv_sum, t

    def arrived(of):
        wait_here(of[0], of[2], *of[3:])

    def product(t, h, r):
        blocks = ext[t * HALVES + h]
        lhs = jnp.concatenate([tiles[r, k] for k in range(kmax)], axis=1)
        rhs = jnp.concatenate([blocks[col[r, k]] for k in range(kmax)], axis=0)
        return jnp.dot(lhs, rhs, preferred_element_type=jnp.float32)

    for r in range(n_rows):
        for copy in load(r):
            copy.wait()
        total = jnp.zeros((bsize, bsize), jnp.float32)
        used = count_ref[0, r]
        for k in range(kmax):
            total += tiles[r, k].astype(jnp.float32) * jnp.where(k < used, 1.0, 0.0)
        deg = jnp.sum(total, axis=1, keepdims=True)
        factor = jnp.broadcast_to(lax.rsqrt(deg), (bsize, half))
        scale[r] = factor
        keep(0, 0, r, (factor * labels[r, :, :half]).astype(jnp.bfloat16))
    pl.semaphore_wait(barrier, n_grp + 1)
    send(*field(0, 0))
    for r in range(n_rows):
        value = (scale[r] * labels[r, :, half:]).astype(jnp.bfloat16)
        keep(0, 1, r, value)
        both = value.astype(jnp.float32) + own[0][r].astype(jnp.float32)
        keep_sum(0, r, jnp.sum(both, axis=1, keepdims=True))
    send(*sums(0))
    send(*field(0, 1))

    def anchor_row(r):
        total = jnp.sum(labels[r, :, :half] + labels[r, :, half:], axis=1, keepdims=True)
        anchor_sum[r] = jnp.broadcast_to(total, (bsize, half))

    for r in range(n_rows):
        anchor_row(r)

    for t in range(ITERS - 1):
        arrived(sums(t))
        arrived(field(t, 0))

        def first_row(r, t=t):
            h_first = product(t, 0, r)
            total = jnp.zeros((bsize, bsize), jnp.float32)
            for k in range(kmax):
                total += tiles[r, k].astype(jnp.float32) * ext_sum[t][col[r, k]]
            total = jnp.broadcast_to(jnp.sum(total, axis=1, keepdims=True), (bsize, half))
            factor = scale[r]
            mean = (0.9 * factor * total + 0.1 * anchor_sum[r]) * (1.0 / classes)
            inverse = factor / mean
            for_h = 0.9 * factor * inverse
            for_l = 0.1 * inverse
            coef_h[r] = for_h
            coef_l[r] = for_l
            value = for_h * h_first + for_l * labels[r, :, :half]
            keep(t + 1, 0, r, value.astype(jnp.bfloat16))

        for r in range(n_rows):
            first_row(r)
        send(*field(t + 1, 0))
        arrived(field(t, 1))

        def second_row(r, t=t):
            value = coef_h[r] * product(t, 1, r) + coef_l[r] * labels[r, :, half:]
            value = value.astype(jnp.bfloat16)
            keep(t + 1, 1, r, value)
            if t + 1 < ITERS - 1:
                both = value.astype(jnp.float32) + own[(t + 1) * HALVES][r].astype(jnp.float32)
                keep_sum(t + 1, r, jnp.sum(both, axis=1, keepdims=True))

        for r in range(n_rows):
            second_row(r)
        if t + 1 < ITERS - 1:
            send(*sums(t + 1))
        send(*field(t + 1, 1))

    last = ITERS - 1

    def update(h, r):
        return 0.9 * scale[r] * product(last, h, r) + 0.1 * labels[r, :, h * half:(h + 1) * half]

    arrived(field(last, 0))

    def last_first(r):
        coef_h[r] = update(0, r)

    for r in range(n_rows):
        last_first(r)
    arrived(field(last, 1))

    def last_second(r):
        second = update(1, r)
        first = coef_h[r]
        mean = jnp.sum(first + second, axis=1, keepdims=True) * (1.0 / classes)
        inverse = jnp.broadcast_to(1.0 / mean, (bsize, half))
        rows = pl.ds(r * bsize, bsize)
        out_ref[0, rows, :half] = first * inverse
        out_ref[0, rows, half:] = second * inverse

    for r in range(n_rows):
        last_second(r)
    for t in range(ITERS):
        if t < ITERS - 1:
            wait_sent(*sums(t))
        for h in range(HALVES):
            wait_sent(*field(t, h))


def solution(mesh):
    n_grp, n_blk = mesh.shape["grp"], mesh.shape["blk"]

    def on_device(labels, tiles, tile_cols, tile_count, send_blocks):
        n_rows, kmax, bsize = tiles.shape[1:4]
        classes = labels.shape[2]
        half = classes // HALVES
        names = n_rows + 2 * HB + n_grp + 1
        count = ITERS * HALVES
        whole = pltpu.VMEM((n_rows, bsize, half), jnp.float32)
        return pl.pallas_call(
            functools.partial(kernel, n_grp, n_blk),
            name="spreading",
            out_shape=pltpu.VMEM(labels.shape, jnp.float32),
            in_specs=[pl.BlockSpec(memory_space=pl.ANY)] * 5,
            out_specs=pl.BlockSpec(memory_space=pltpu.VMEM),
            scratch_shapes=[pltpu.VMEM((names, bsize, half), jnp.bfloat16)] * count
            + [pltpu.VMEM((n_rows, bsize, half), jnp.bfloat16)] * count
            + [pltpu.VMEM((n_grp, bsize, half), jnp.bfloat16)] * count
            + [pltpu.VMEM((names, 1, bsize), jnp.float32)] * (ITERS - 1)
            + [pltpu.VMEM((n_rows, 1, bsize), jnp.float32)] * (ITERS - 1)
            + [pltpu.VMEM((n_grp, 1, bsize), jnp.float32)] * (ITERS - 1)
            + [
                pltpu.VMEM((n_rows, kmax, bsize, bsize), jnp.bfloat16),
                pltpu.VMEM((n_rows, bsize, classes), jnp.float32),
                whole,
                whole,
                whole,
                whole,
                pltpu.SMEM((1, n_rows, kmax), jnp.int32),
                pltpu.SMEM((1, n_rows), jnp.int32),
                pltpu.SMEM((1, 1, n_grp), jnp.int32),
                pltpu.SMEM((n_rows, kmax), jnp.int32),
                pltpu.SemaphoreType.DMA((2 * n_rows,)),
                pltpu.SemaphoreType.DMA((3,)),
                pltpu.SemaphoreType.DMA((count, 3)),
                pltpu.SemaphoreType.DMA((count, 3)),
                pltpu.SemaphoreType.DMA((ITERS - 1, 3)),
                pltpu.SemaphoreType.DMA((ITERS - 1, 3)),
            ],
            compiler_params=pltpu.CompilerParams(
                collective_id=0, has_side_effects=True, vmem_limit_bytes=32 << 20
            ),
        )(*(
            pltpu.with_memory_space_constraint(a, pltpu.HBM)
            for a in (tile_cols, tile_count, send_blocks.reshape(1, 1, n_grp), labels, tiles)
        ))

    return jax.shard_map(
        on_device,
        mesh=mesh,
        in_specs=(
            P("grp", "blk", None),
            P("grp", "blk", None, None, None),
            P("grp", "blk", None),
            P("grp", "blk"),
            P("grp", "blk", None, None),
        ),
        out_specs=P("grp", "blk", None),
        check_vma=False,
    )
```

```python
import functools

import jax
import jax.numpy as jnp
from jax import lax
from jax.experimental import pallas as pl
from jax.experimental.pallas import tpu as pltpu
from jax.sharding import PartitionSpec as P

HB = 2
ITERS = 3
HALVES = 2
PIECE = 64
ORDER = (
    (2, 2), (0, 1), (1, 2), (3, 0), (2, 1), (0, 3), (3, 2), (1, 0), (2, 3), (1, 1), (3, 3), (0, 2), (1, 3), (3, 1), (2, 0),
)
MESH = pl.DeviceIdType.MESH


def kernel(n_grp, n_blk, cols_hbm, count_hbm, pick_hbm, labels_hbm, tiles_hbm, out_ref, *scratch):
    ext = scratch[0:6]
    own = scratch[6:12]
    staged = scratch[12:18]
    ext_sum = scratch[18:20]
    own_sum = scratch[20:22]
    staged_sum = scratch[22:24]
    (tiles, labels, scale, anchor_sum, coef_h, coef_l, cols_ref, count_ref, pick_ref, col, load_sem, small_sem, send_sem, recv_sem,
     send_sum, recv_sum) = scratch[24:]
    n_rows, kmax, bsize = tiles.shape[0], tiles.shape[1], tiles.shape[2]
    classes = labels.shape[2]
    half = classes // HALVES
    local = n_rows + 2 * HB
    zero = local + n_grp
    me = lax.axis_index("grp")
    place = lax.axis_index("blk")
    after = lax.rem(place + 1, n_blk)
    before = lax.rem(place + n_blk - 1, n_blk)

    def load(r):
        return (
            pltpu.make_async_copy(tiles_hbm.at[0, r], tiles.at[r], load_sem.at[r]),
            pltpu.make_async_copy(labels_hbm.at[0, pl.ds(r * bsize, bsize)], labels.at[r], load_sem.at[n_rows + r]),
        )

    if n_grp == 16:
        y, x = lax.div(me, 4), lax.rem(me, 4)
        others = [lax.rem(y + dy, 4) * 4 + lax.rem(x + dx, 4) for dy, dx in ORDER]
    else:
        others = [lax.rem(me + p, n_grp) for p in range(1, n_grp)]

    barrier = pltpu.get_barrier_semaphore()
    for other in others:
        pl.semaphore_signal(barrier, inc=1, device_id={"grp": other}, device_id_type=MESH)
    pl.semaphore_signal(barrier, inc=1, device_id={"blk": after}, device_id_type=MESH)
    pl.semaphore_signal(barrier, inc=1, device_id={"blk": before}, device_id_type=MESH)

    small = [
        pltpu.make_async_copy(src, dst, small_sem.at[i])
        for i, (src, dst) in enumerate(((cols_hbm, cols_ref), (count_hbm, count_ref), (pick_hbm, pick_ref)))
    ]
    for copy in small:
        copy.start()
    for r in range(n_rows):
        for copy in load(r):
            copy.start()

    def name_row(r, carry):
        used = count_ref[0, r]
        for k in range(kmax):
            c = cols_ref[0, r, k]
            block = place * n_rows + c - HB
            outside = (c < local) & ((block < 0) | (block >= n_blk * n_rows))
            col[r, k] = jnp.where((k < used) & jnp.logical_not(outside), c, zero)
        return carry

    for copy in small:
        copy.wait()
    lax.fori_loop(0, n_rows, name_row, 0)
    for ref in ext:
        ref[zero] = jnp.zeros((bsize, half), jnp.bfloat16)
    for ref in ext_sum:
        ref[zero] = jnp.zeros((1, bsize), jnp.float32)

    def keep(t, h, r, value):
        own[t * HALVES + h][r] = value
        ext[t * HALVES + h][HB + r] = value

    def keep_sum(t, r, total):
        at_row = lax.broadcasted_iota(jnp.int32, (bsize, bsize), 0)
        at_col = lax.broadcasted_iota(jnp.int32, (bsize, bsize), 1)
        spread = jnp.where(at_row == at_col, jnp.broadcast_to(total, (bsize, bsize)), 0.0)
        row = jnp.sum(spread, axis=0, keepdims=True)
        own_sum[t][r] = row
        ext_sum[t][HB + r] = row

    def halo_copies(mine, theirs, ssem, rsem, t):
        return (
            pltpu.make_async_remote_copy(
                src_ref=mine.at[pl.ds(n_rows - HB, HB)], dst_ref=theirs.at[pl.ds(0, HB)],
                send_sem=ssem.at[t, 1], recv_sem=rsem.at[t, 1], device_id={"blk": after}, device_id_type=MESH,
            ),
            pltpu.make_async_remote_copy(
                src_ref=mine.at[pl.ds(0, HB)], dst_ref=theirs.at[pl.ds(HB + n_rows, HB)],
                send_sem=ssem.at[t, 2], recv_sem=rsem.at[t, 2], device_id={"blk": before}, device_id_type=MESH,
            ),
        )

    def send(mine, out, theirs, ssem, rsem, t):
        height = mine.shape[1]
        piece = min(PIECE, height)
        for first in range(0, height, piece):
            rows = pl.ds(first, piece)
            for i, other in enumerate(others):
                if first == 0:
                    out[i] = mine[pick_ref[0, 0, other]]
                pltpu.make_async_remote_copy(
                    src_ref=out.at[i, rows], dst_ref=theirs.at[local + me, rows],
                    send_sem=ssem.at[t, 0], recv_sem=rsem.at[t, 0], device_id={"grp": other}, device_id_type=MESH,
                ).start()
        for copy in halo_copies(mine, theirs, ssem, rsem, t):
            copy.start()
        theirs[local + me] = mine[pick_ref[0, 0, me]]

    def wait_sent(mine, out, theirs, ssem, rsem, t):
        whole = out.at[pl.ds(0, n_grp - 1)]
        pltpu.make_async_copy(whole, whole, ssem.at[t, 0]).wait()
        for copy in halo_copies(mine, theirs, ssem, rsem, t):
            copy.wait_send()

    def wait_here(mine, theirs, ssem, rsem, t):
        whole = theirs.at[pl.ds(local, n_grp - 1)]
        pltpu.make_async_copy(whole, whole, rsem.at[t, 0]).wait()
        for copy in halo_copies(mine, theirs, ssem, rsem, t):
            copy.wait_recv()

    def field(t, h):
        i = t * HALVES + h
        return own[i], staged[i], ext[i], send_sem, recv_sem, i

    def sums(t):
        return own_sum[t], staged_sum[t], ext_sum[t], send_sum, recv_sum, t

    def arrived(of):
        wait_here(of[0], of[2], *of[3:])

    def product(t, h, r):
        blocks = ext[t * HALVES + h]
        lhs = jnp.concatenate([tiles[r, k] for k in range(kmax)], axis=1)
        rhs = jnp.concatenate([blocks[col[r, k]] for k in range(kmax)], axis=0)
        return jnp.dot(lhs, rhs, preferred_element_type=jnp.float32)

    for r in range(n_rows):
        for copy in load(r):
            copy.wait()
        total = jnp.zeros((bsize, bsize), jnp.float32)
        used = count_ref[0, r]
        for k in range(kmax):
            total += tiles[r, k].astype(jnp.float32) * jnp.where(k < used, 1.0, 0.0)
        deg = jnp.sum(total, axis=1, keepdims=True)
        factor = jnp.broadcast_to(lax.rsqrt(deg), (bsize, half))
        scale[r] = factor
        keep(0, 0, r, (factor * labels[r, :, :half]).astype(jnp.bfloat16))
    pl.semaphore_wait(barrier, n_grp + 1)
    send(*field(0, 0))
    for r in range(n_rows):
        value = (scale[r] * labels[r, :, half:]).astype(jnp.bfloat16)
        keep(0, 1, r, value)
        both = value.astype(jnp.float32) + own[0][r].astype(jnp.float32)
        keep_sum(0, r, jnp.sum(both, axis=1, keepdims=True))
    send(*sums(0))
    send(*field(0, 1))

    def anchor_row(r):
        total = jnp.sum(labels[r, :, :half] + labels[r, :, half:], axis=1, keepdims=True)
        anchor_sum[r] = jnp.broadcast_to(total, (bsize, half))

    for r in range(n_rows):
        anchor_row(r)

    for t in range(ITERS - 1):
        arrived(sums(t))
        arrived(field(t, 0))

        def first_row(r, t=t):
            h_first = product(t, 0, r)
            total = jnp.zeros((bsize, bsize), jnp.float32)
            for k in range(kmax):
                total += tiles[r, k].astype(jnp.float32) * ext_sum[t][col[r, k]]
            total = jnp.broadcast_to(jnp.sum(total, axis=1, keepdims=True), (bsize, half))
            factor = scale[r]
            mean = (0.9 * factor * total + 0.1 * anchor_sum[r]) * (1.0 / classes)
            inverse = factor / mean
            for_h = 0.9 * factor * inverse
            for_l = 0.1 * inverse
            coef_h[r] = for_h
            coef_l[r] = for_l
            value = for_h * h_first + for_l * labels[r, :, :half]
            keep(t + 1, 0, r, value.astype(jnp.bfloat16))

        for r in range(n_rows):
            first_row(r)
        send(*field(t + 1, 0))
        arrived(field(t, 1))

        def second_row(r, t=t):
            value = coef_h[r] * product(t, 1, r) + coef_l[r] * labels[r, :, half:]
            value = value.astype(jnp.bfloat16)
            keep(t + 1, 1, r, value)
            if t + 1 < ITERS - 1:
                both = value.astype(jnp.float32) + own[(t + 1) * HALVES][r].astype(jnp.float32)
                keep_sum(t + 1, r, jnp.sum(both, axis=1, keepdims=True))

        for r in range(n_rows):
            second_row(r)
        if t + 1 < ITERS - 1:
            send(*sums(t + 1))
        send(*field(t + 1, 1))

    last = ITERS - 1

    def update(h, r):
        return 0.9 * scale[r] * product(last, h, r) + 0.1 * labels[r, :, h * half:(h + 1) * half]

    arrived(field(last, 0))

    def last_first(r):
        coef_h[r] = update(0, r)

    for r in range(n_rows):
        last_first(r)
    arrived(field(last, 1))

    def last_second(r):
        second = update(1, r)
        first = coef_h[r]
        mean = jnp.sum(first + second, axis=1, keepdims=True) * (1.0 / classes)
        inverse = jnp.broadcast_to(1.0 / mean, (bsize, half))
        rows = pl.ds(r * bsize, bsize)
        out_ref[0, rows, :half] = first * inverse
        out_ref[0, rows, half:] = second * inverse

    for r in range(n_rows):
        last_second(r)
    for t in range(ITERS):
        if t < ITERS - 1:
            wait_sent(*sums(t))
        for h in range(HALVES):
            wait_sent(*field(t, h))


def solution(mesh):
    n_grp, n_blk = mesh.shape["grp"], mesh.shape["blk"]

    def on_device(labels, tiles, tile_cols, tile_count, send_blocks):
        n_rows, kmax, bsize = tiles.shape[1:4]
        classes = labels.shape[2]
        half = classes // HALVES
        names = n_rows + 2 * HB + n_grp + 1
        count = ITERS * HALVES
        whole = pltpu.VMEM((n_rows, bsize, half), jnp.float32)
        return pl.pallas_call(
            functools.partial(kernel, n_grp, n_blk),
            name="spreading",
            out_shape=pltpu.VMEM(labels.shape, jnp.float32),
            in_specs=[pl.BlockSpec(memory_space=pl.ANY)] * 5,
            out_specs=pl.BlockSpec(memory_space=pltpu.VMEM),
            scratch_shapes=[pltpu.VMEM((names, bsize, half), jnp.bfloat16)] * count
            + [pltpu.VMEM((n_rows, bsize, half), jnp.bfloat16)] * count
            + [pltpu.VMEM((n_grp - 1, bsize, half), jnp.bfloat16)] * count
            + [pltpu.VMEM((names, 1, bsize), jnp.float32)] * (ITERS - 1)
            + [pltpu.VMEM((n_rows, 1, bsize), jnp.float32)] * (ITERS - 1)
            + [pltpu.VMEM((n_grp - 1, 1, bsize), jnp.float32)] * (ITERS - 1)
            + [
                pltpu.VMEM((n_rows, kmax, bsize, bsize), jnp.bfloat16),
                pltpu.VMEM((n_rows, bsize, classes), jnp.float32),
                whole,
                whole,
                whole,
                whole,
                pltpu.SMEM((1, n_rows, kmax), jnp.int32),
                pltpu.SMEM((1, n_rows), jnp.int32),
                pltpu.SMEM((1, 1, n_grp), jnp.int32),
                pltpu.SMEM((n_rows, kmax), jnp.int32),
                pltpu.SemaphoreType.DMA((2 * n_rows,)),
                pltpu.SemaphoreType.DMA((3,)),
                pltpu.SemaphoreType.DMA((count, 3)),
                pltpu.SemaphoreType.DMA((count, 3)),
                pltpu.SemaphoreType.DMA((ITERS - 1, 3)),
                pltpu.SemaphoreType.DMA((ITERS - 1, 3)),
            ],
            compiler_params=pltpu.CompilerParams(
                collective_id=0, has_side_effects=True, vmem_limit_bytes=32 << 20
            ),
        )(*(
            pltpu.with_memory_space_constraint(a, pltpu.HBM)
            for a in (tile_cols, tile_count, send_blocks.reshape(1, 1, n_grp), labels, tiles)
        ))

    return jax.shard_map(
        on_device,
        mesh=mesh,
        in_specs=(
            P("grp", "blk", None),
            P("grp", "blk", None, None, None),
            P("grp", "blk", None),
            P("grp", "blk"),
            P("grp", "blk", None, None),
        ),
        out_specs=P("grp", "blk", None),
        check_vma=False,
    )
```

```python
import functools

import jax
import jax.numpy as jnp
from jax import lax
from jax.experimental import pallas as pl
from jax.experimental.pallas import tpu as pltpu
from jax.sharding import PartitionSpec as P

HB = 2
ITERS = 3
HALVES = 2
PIECE = 64
ORDER = (
    (2, 2), (0, 1), (1, 2), (3, 0), (2, 1), (0, 3), (3, 2), (1, 0), (2, 3), (1, 1), (3, 3), (0, 2), (1, 3), (3, 1), (2, 0),
)
MESH = pl.DeviceIdType.MESH


def kernel(n_grp, n_blk, cols_hbm, count_hbm, pick_hbm, labels_hbm, tiles_hbm, out_ref, *scratch):
    ext = scratch[0:6]
    own = scratch[6:12]
    staged = scratch[12:18]
    ext_sum = scratch[18:20]
    own_sum = scratch[20:22]
    staged_sum = scratch[22:24]
    (tiles, labels, scale, anchor_sum, coef_h, coef_l, cols_ref, count_ref, pick_ref, col, load_sem, small_sem, send_sem, recv_sem,
     send_sum, recv_sum) = scratch[24:]
    n_rows, kmax, bsize = tiles.shape[0], tiles.shape[1], tiles.shape[2]
    classes = labels.shape[2]
    half = classes // HALVES
    local = n_rows + 2 * HB
    zero = local + n_grp
    me = lax.axis_index("grp")
    place = lax.axis_index("blk")
    after = lax.rem(place + 1, n_blk)
    before = lax.rem(place + n_blk - 1, n_blk)

    def load(r):
        return (
            pltpu.make_async_copy(tiles_hbm.at[0, r], tiles.at[r], load_sem.at[r]),
            pltpu.make_async_copy(labels_hbm.at[0, pl.ds(r * bsize, bsize)], labels.at[r], load_sem.at[n_rows + r]),
        )

    small = [
        pltpu.make_async_copy(src, dst, small_sem.at[i])
        for i, (src, dst) in enumerate(((cols_hbm, cols_ref), (count_hbm, count_ref), (pick_hbm, pick_ref)))
    ]
    for copy in small:
        copy.start()
    for r in range(n_rows):
        for copy in load(r):
            copy.start()

    if n_grp == 16:
        y, x = lax.div(me, 4), lax.rem(me, 4)
        others = [lax.rem(y + dy, 4) * 4 + lax.rem(x + dx, 4) for dy, dx in ORDER]
    else:
        others = [lax.rem(me + p, n_grp) for p in range(1, n_grp)]

    barrier = pltpu.get_barrier_semaphore()
    for other in others:
        pl.semaphore_signal(barrier, inc=1, device_id={"grp": other}, device_id_type=MESH)
    pl.semaphore_signal(barrier, inc=1, device_id={"blk": after}, device_id_type=MESH)
    pl.semaphore_signal(barrier, inc=1, device_id={"blk": before}, device_id_type=MESH)

    def name_row(r, carry):
        used = count_ref[0, r]
        for k in range(kmax):
            c = cols_ref[0, r, k]
            block = place * n_rows + c - HB
            outside = (c < local) & ((block < 0) | (block >= n_blk * n_rows))
            col[r, k] = jnp.where((k < used) & jnp.logical_not(outside), c, zero)
        return carry

    for copy in small:
        copy.wait()
    lax.fori_loop(0, n_rows, name_row, 0)
    for ref in ext:
        ref[zero] = jnp.zeros((bsize, half), jnp.bfloat16)
    for ref in ext_sum:
        ref[zero] = jnp.zeros((1, bsize), jnp.float32)

    def keep(t, h, r, value):
        own[t * HALVES + h][r] = value
        ext[t * HALVES + h][HB + r] = value

    def keep_sum(t, r, total):
        at_row = lax.broadcasted_iota(jnp.int32, (bsize, bsize), 0)
        at_col = lax.broadcasted_iota(jnp.int32, (bsize, bsize), 1)
        spread = jnp.where(at_row == at_col, jnp.broadcast_to(total, (bsize, bsize)), 0.0)
        row = jnp.sum(spread, axis=0, keepdims=True)
        own_sum[t][r] = row
        ext_sum[t][HB + r] = row

    def halo_copies(mine, theirs, ssem, rsem, t):
        return (
            pltpu.make_async_remote_copy(
                src_ref=mine.at[pl.ds(n_rows - HB, HB)], dst_ref=theirs.at[pl.ds(0, HB)],
                send_sem=ssem.at[t, 1], recv_sem=rsem.at[t, 1], device_id={"blk": after}, device_id_type=MESH,
            ),
            pltpu.make_async_remote_copy(
                src_ref=mine.at[pl.ds(0, HB)], dst_ref=theirs.at[pl.ds(HB + n_rows, HB)],
                send_sem=ssem.at[t, 2], recv_sem=rsem.at[t, 2], device_id={"blk": before}, device_id_type=MESH,
            ),
        )

    def send(mine, out, theirs, ssem, rsem, t):
        height = mine.shape[1]
        piece = min(PIECE, height)
        for first in range(0, height, piece):
            rows = pl.ds(first, piece)
            for i, other in enumerate(others):
                if first == 0:
                    out[i] = mine[pick_ref[0, 0, other]]
                pltpu.make_async_remote_copy(
                    src_ref=out.at[i, rows], dst_ref=theirs.at[local + me, rows],
                    send_sem=ssem.at[t, 0], recv_sem=rsem.at[t, 0], device_id={"grp": other}, device_id_type=MESH,
                ).start()
        for copy in halo_copies(mine, theirs, ssem, rsem, t):
            copy.start()
        theirs[local + me] = mine[pick_ref[0, 0, me]]

    def wait_sent(mine, out, theirs, ssem, rsem, t):
        whole = out.at[pl.ds(0, n_grp - 1)]
        pltpu.make_async_copy(whole, whole, ssem.at[t, 0]).wait()
        for copy in halo_copies(mine, theirs, ssem, rsem, t):
            copy.wait_send()

    def wait_here(mine, theirs, ssem, rsem, t):
        whole = theirs.at[pl.ds(local, n_grp - 1)]
        pltpu.make_async_copy(whole, whole, rsem.at[t, 0]).wait()
        for copy in halo_copies(mine, theirs, ssem, rsem, t):
            copy.wait_recv()

    def field(t, h):
        i = t * HALVES + h
        return own[i], staged[i], ext[i], send_sem, recv_sem, i

    def sums(t):
        return own_sum[t], staged_sum[t], ext_sum[t], send_sum, recv_sum, t

    def arrived(of):
        wait_here(of[0], of[2], *of[3:])

    def product(t, h, r):
        blocks = ext[t * HALVES + h]
        lhs = jnp.concatenate([tiles[r, k] for k in range(kmax)], axis=1)
        rhs = jnp.concatenate([blocks[col[r, k]] for k in range(kmax)], axis=0)
        return jnp.dot(lhs, rhs, preferred_element_type=jnp.float32)

    for r in range(n_rows):
        for copy in load(r):
            copy.wait()
        total = jnp.zeros((bsize, bsize), jnp.float32)
        used = count_ref[0, r]
        for k in range(kmax):
            total += tiles[r, k].astype(jnp.float32) * jnp.where(k < used, 1.0, 0.0)
        deg = jnp.sum(total, axis=1, keepdims=True)
        factor = jnp.broadcast_to(lax.rsqrt(deg), (bsize, half))
        scale[r] = factor
        keep(0, 0, r, (factor * labels[r, :, :half]).astype(jnp.bfloat16))
    pl.semaphore_wait(barrier, n_grp + 1)
    send(*field(0, 0))
    for r in range(n_rows):
        value = (scale[r] * labels[r, :, half:]).astype(jnp.bfloat16)
        keep(0, 1, r, value)
        both = value.astype(jnp.float32) + own[0][r].astype(jnp.float32)
        keep_sum(0, r, jnp.sum(both, axis=1, keepdims=True))
    send(*sums(0))
    send(*field(0, 1))

    def anchor_row(r):
        total = jnp.sum(labels[r, :, :half] + labels[r, :, half:], axis=1, keepdims=True)
        anchor_sum[r] = jnp.broadcast_to(total, (bsize, half))

    for r in range(n_rows):
        anchor_row(r)

    for t in range(ITERS - 1):
        arrived(sums(t))
        arrived(field(t, 0))

        def first_row(r, t=t):
            h_first = product(t, 0, r)
            total = jnp.zeros((bsize, bsize), jnp.float32)
            for k in range(kmax):
                total += tiles[r, k].astype(jnp.float32) * ext_sum[t][col[r, k]]
            total = jnp.broadcast_to(jnp.sum(total, axis=1, keepdims=True), (bsize, half))
            factor = scale[r]
            mean = (0.9 * factor * total + 0.1 * anchor_sum[r]) * (1.0 / classes)
            inverse = factor / mean
            for_h = 0.9 * factor * inverse
            for_l = 0.1 * inverse
            coef_h[r] = for_h
            coef_l[r] = for_l
            value = for_h * h_first + for_l * labels[r, :, :half]
            keep(t + 1, 0, r, value.astype(jnp.bfloat16))

        for r in range(n_rows):
            first_row(r)
        send(*field(t + 1, 0))
        arrived(field(t, 1))

        def second_row(r, t=t):
            value = coef_h[r] * product(t, 1, r) + coef_l[r] * labels[r, :, half:]
            value = value.astype(jnp.bfloat16)
            keep(t + 1, 1, r, value)
            if t + 1 < ITERS - 1:
                both = value.astype(jnp.float32) + own[(t + 1) * HALVES][r].astype(jnp.float32)
                keep_sum(t + 1, r, jnp.sum(both, axis=1, keepdims=True))

        for r in range(n_rows):
            second_row(r)
        if t + 1 < ITERS - 1:
            send(*sums(t + 1))
        send(*field(t + 1, 1))

    last = ITERS - 1

    def update(h, r):
        return 0.9 * scale[r] * product(last, h, r) + 0.1 * labels[r, :, h * half:(h + 1) * half]

    arrived(field(last, 0))

    def last_first(r):
        coef_h[r] = update(0, r)

    for r in range(n_rows):
        last_first(r)
    arrived(field(last, 1))

    def last_second(r):
        second = update(1, r)
        first = coef_h[r]
        mean = jnp.sum(first + second, axis=1, keepdims=True) * (1.0 / classes)
        inverse = jnp.broadcast_to(1.0 / mean, (bsize, half))
        rows = pl.ds(r * bsize, bsize)
        out_ref[0, rows, :half] = first * inverse
        out_ref[0, rows, half:] = second * inverse

    for r in range(n_rows):
        last_second(r)
    for t in range(ITERS):
        if t < ITERS - 1:
            wait_sent(*sums(t))
        for h in range(HALVES):
            wait_sent(*field(t, h))


def solution(mesh):
    n_grp, n_blk = mesh.shape["grp"], mesh.shape["blk"]

    def on_device(labels, tiles, tile_cols, tile_count, send_blocks):
        n_rows, kmax, bsize = tiles.shape[1:4]
        classes = labels.shape[2]
        half = classes // HALVES
        names = n_rows + 2 * HB + n_grp + 1
        count = ITERS * HALVES
        whole = pltpu.VMEM((n_rows, bsize, half), jnp.float32)
        return pl.pallas_call(
            functools.partial(kernel, n_grp, n_blk),
            name="spreading",
            out_shape=pltpu.VMEM(labels.shape, jnp.float32),
            in_specs=[pl.BlockSpec(memory_space=pl.ANY)] * 5,
            out_specs=pl.BlockSpec(memory_space=pltpu.VMEM),
            scratch_shapes=[pltpu.VMEM((names, bsize, half), jnp.bfloat16)] * count
            + [pltpu.VMEM((n_rows, bsize, half), jnp.bfloat16)] * count
            + [pltpu.VMEM((n_grp - 1, bsize, half), jnp.bfloat16)] * count
            + [pltpu.VMEM((names, 1, bsize), jnp.float32)] * (ITERS - 1)
            + [pltpu.VMEM((n_rows, 1, bsize), jnp.float32)] * (ITERS - 1)
            + [pltpu.VMEM((n_grp - 1, 1, bsize), jnp.float32)] * (ITERS - 1)
            + [
                pltpu.VMEM((n_rows, kmax, bsize, bsize), jnp.bfloat16),
                pltpu.VMEM((n_rows, bsize, classes), jnp.float32),
                whole,
                whole,
                whole,
                whole,
                pltpu.SMEM((1, n_rows, kmax), jnp.int32),
                pltpu.SMEM((1, n_rows), jnp.int32),
                pltpu.SMEM((1, 1, n_grp), jnp.int32),
                pltpu.SMEM((n_rows, kmax), jnp.int32),
                pltpu.SemaphoreType.DMA((2 * n_rows,)),
                pltpu.SemaphoreType.DMA((3,)),
                pltpu.SemaphoreType.DMA((count, 3)),
                pltpu.SemaphoreType.DMA((count, 3)),
                pltpu.SemaphoreType.DMA((ITERS - 1, 3)),
                pltpu.SemaphoreType.DMA((ITERS - 1, 3)),
            ],
            compiler_params=pltpu.CompilerParams(
                collective_id=0, has_side_effects=True, vmem_limit_bytes=32 << 20
            ),
        )(*(
            pltpu.with_memory_space_constraint(a, pltpu.HBM)
            for a in (tile_cols, tile_count, send_blocks.reshape(1, 1, n_grp), labels, tiles)
        ))

    return jax.shard_map(
        on_device,
        mesh=mesh,
        in_specs=(
            P("grp", "blk", None),
            P("grp", "blk", None, None, None),
            P("grp", "blk", None),
            P("grp", "blk"),
            P("grp", "blk", None, None),
        ),
        out_specs=P("grp", "blk", None),
        check_vma=False,
    )
```

```python
import functools

import jax
import jax.numpy as jnp
from jax import lax
from jax.experimental import pallas as pl
from jax.experimental.pallas import tpu as pltpu
from jax.sharding import PartitionSpec as P

HB = 2
ITERS = 3
HALVES = 2
PIECE = 64
ORDER = (
    (2, 2), (0, 1), (1, 2), (3, 0), (2, 1), (0, 3), (3, 2), (1, 0), (2, 3), (1, 1), (3, 3), (0, 2), (1, 3), (3, 1), (2, 0),
)
MESH = pl.DeviceIdType.MESH


def kernel(n_grp, n_blk, cols_hbm, count_hbm, pick_hbm, labels_hbm, tiles_hbm, out_ref, *scratch):
    ext = scratch[0:6]
    own = scratch[6:12]
    staged = scratch[12:18]
    ext_sum = scratch[18:20]
    own_sum = scratch[20:22]
    staged_sum = scratch[22:24]
    (tiles, labels, scale, anchor_sum, coef_h, coef_l, cols_ref, count_ref, pick_ref, col, load_sem, small_sem, send_sem, recv_sem,
     send_sum, recv_sum) = scratch[24:]
    n_rows, kmax, bsize = tiles.shape[0], tiles.shape[1], tiles.shape[2]
    classes = labels.shape[2]
    half = classes // HALVES
    local = n_rows + 2 * HB
    zero = local + n_grp
    me = lax.axis_index("grp")
    place = lax.axis_index("blk")
    after = lax.rem(place + 1, n_blk)
    before = lax.rem(place + n_blk - 1, n_blk)

    def load(r):
        return (
            pltpu.make_async_copy(tiles_hbm.at[0, r], tiles.at[r], load_sem.at[r]),
            pltpu.make_async_copy(labels_hbm.at[0, pl.ds(r * bsize, bsize)], labels.at[r], load_sem.at[n_rows + r]),
        )

    if n_grp == 16:
        y, x = lax.div(me, 4), lax.rem(me, 4)
        others = [lax.rem(y + dy, 4) * 4 + lax.rem(x + dx, 4) for dy, dx in ORDER]
    else:
        others = [lax.rem(me + p, n_grp) for p in range(1, n_grp)]

    barrier = pltpu.get_barrier_semaphore()
    for other in others:
        pl.semaphore_signal(barrier, inc=1, device_id={"grp": other}, device_id_type=MESH)
    pl.semaphore_signal(barrier, inc=1, device_id={"blk": after}, device_id_type=MESH)
    pl.semaphore_signal(barrier, inc=1, device_id={"blk": before}, device_id_type=MESH)

    small = [
        pltpu.make_async_copy(src, dst, small_sem.at[i])
        for i, (src, dst) in enumerate(((cols_hbm, cols_ref), (count_hbm, count_ref), (pick_hbm, pick_ref)))
    ]
    for copy in small:
        copy.start()
    for r in range(n_rows):
        for copy in load(r):
            copy.start()

    def name_row(r, carry):
        used = count_ref[0, r]
        for k in range(kmax):
            c = cols_ref[0, r, k]
            block = place * n_rows + c - HB
            outside = (c < local) & ((block < 0) | (block >= n_blk * n_rows))
            col[r, k] = jnp.where((k < used) & jnp.logical_not(outside), c, zero)
        return carry

    for copy in small:
        copy.wait()
    lax.fori_loop(0, n_rows, name_row, 0)
    for ref in ext:
        ref[zero] = jnp.zeros((bsize, half), jnp.bfloat16)
    for ref in ext_sum:
        ref[zero] = jnp.zeros((1, bsize), jnp.float32)

    def keep(t, h, r, value):
        own[t * HALVES + h][r] = value
        ext[t * HALVES + h][HB + r] = value

    def keep_sum(t, r, total):
        at_row = lax.broadcasted_iota(jnp.int32, (bsize, bsize), 0)
        at_col = lax.broadcasted_iota(jnp.int32, (bsize, bsize), 1)
        spread = jnp.where(at_row == at_col, jnp.broadcast_to(total, (bsize, bsize)), 0.0)
        row = jnp.sum(spread, axis=0, keepdims=True)
        own_sum[t][r] = row
        ext_sum[t][HB + r] = row

    def halo_copies(mine, theirs, ssem, rsem, t):
        return (
            pltpu.make_async_remote_copy(
                src_ref=mine.at[pl.ds(n_rows - HB, HB)], dst_ref=theirs.at[pl.ds(0, HB)],
                send_sem=ssem.at[t, 1], recv_sem=rsem.at[t, 1], device_id={"blk": after}, device_id_type=MESH,
            ),
            pltpu.make_async_remote_copy(
                src_ref=mine.at[pl.ds(0, HB)], dst_ref=theirs.at[pl.ds(HB + n_rows, HB)],
                send_sem=ssem.at[t, 2], recv_sem=rsem.at[t, 2], device_id={"blk": before}, device_id_type=MESH,
            ),
        )

    def send(mine, out, theirs, ssem, rsem, t):
        height = mine.shape[1]
        piece = min(PIECE, height)
        for first in range(0, height, piece):
            rows = pl.ds(first, piece)
            for i, other in enumerate(others):
                if first == 0:
                    out[i] = mine[pick_ref[0, 0, other]]
                pltpu.make_async_remote_copy(
                    src_ref=out.at[i, rows], dst_ref=theirs.at[local + me, rows],
                    send_sem=ssem.at[t, 0], recv_sem=rsem.at[t, 0], device_id={"grp": other}, device_id_type=MESH,
                ).start()
        for copy in halo_copies(mine, theirs, ssem, rsem, t):
            copy.start()
        theirs[local + me] = mine[pick_ref[0, 0, me]]

    def wait_sent(mine, out, theirs, ssem, rsem, t):
        whole = out.at[pl.ds(0, n_grp - 1)]
        pltpu.make_async_copy(whole, whole, ssem.at[t, 0]).wait()
        for copy in halo_copies(mine, theirs, ssem, rsem, t):
            copy.wait_send()

    def wait_here(mine, theirs, ssem, rsem, t):
        whole = theirs.at[pl.ds(local, n_grp - 1)]
        pltpu.make_async_copy(whole, whole, rsem.at[t, 0]).wait()
        for copy in halo_copies(mine, theirs, ssem, rsem, t):
            copy.wait_recv()

    def field(t, h):
        i = t * HALVES + h
        return own[i], staged[i], ext[i], send_sem, recv_sem, i

    def sums(t):
        return own_sum[t], staged_sum[t], ext_sum[t], send_sum, recv_sum, t

    def arrived(of):
        wait_here(of[0], of[2], *of[3:])

    def product(t, h, r):
        blocks = ext[t * HALVES + h]
        lhs = jnp.concatenate([tiles[r, k] for k in range(kmax)], axis=1)
        rhs = jnp.concatenate([blocks[col[r, k]] for k in range(kmax)], axis=0)
        return jnp.dot(lhs, rhs, preferred_element_type=jnp.float32)

    for r in range(n_rows):
        for copy in load(r):
            copy.wait()
        total = jnp.zeros((bsize, bsize), jnp.float32)
        used = count_ref[0, r]
        for k in range(kmax // 2):
            total += tiles[r, k].astype(jnp.float32) * jnp.where(k < used, 1.0, 0.0)
        later = range(kmax // 2, kmax)
        ones = [jnp.broadcast_to(jnp.where(k < used, 1.0, 0.0), (bsize, half)).astype(jnp.bfloat16) for k in later]
        deg = jnp.sum(total, axis=1, keepdims=True) + jnp.dot(
            jnp.concatenate([tiles[r, k] for k in later], axis=1),
            jnp.concatenate(ones, axis=0),
            preferred_element_type=jnp.float32,
        )
        factor = lax.rsqrt(deg)
        scale[r] = factor
        keep(0, 0, r, (factor * labels[r, :, :half]).astype(jnp.bfloat16))
    pl.semaphore_wait(barrier, n_grp + 1)
    send(*field(0, 0))
    for r in range(n_rows):
        value = (scale[r] * labels[r, :, half:]).astype(jnp.bfloat16)
        keep(0, 1, r, value)
        both = value.astype(jnp.float32) + own[0][r].astype(jnp.float32)
        keep_sum(0, r, jnp.sum(both, axis=1, keepdims=True))
    send(*sums(0))
    send(*field(0, 1))

    def anchor_row(r):
        total = jnp.sum(labels[r, :, :half] + labels[r, :, half:], axis=1, keepdims=True)
        anchor_sum[r] = jnp.broadcast_to(total, (bsize, half))

    for r in range(n_rows):
        anchor_row(r)

    for t in range(ITERS - 1):
        arrived(sums(t))
        arrived(field(t, 0))

        def first_row(r, t=t):
            h_first = product(t, 0, r)
            total = jnp.zeros((bsize, bsize), jnp.float32)
            for k in range(kmax):
                total += tiles[r, k].astype(jnp.float32) * ext_sum[t][col[r, k]]
            total = jnp.broadcast_to(jnp.sum(total, axis=1, keepdims=True), (bsize, half))
            factor = scale[r]
            mean = (0.9 * factor * total + 0.1 * anchor_sum[r]) * (1.0 / classes)
            inverse = factor / mean
            for_h = 0.9 * factor * inverse
            for_l = 0.1 * inverse
            coef_h[r] = for_h
            coef_l[r] = for_l
            value = for_h * h_first + for_l * labels[r, :, :half]
            keep(t + 1, 0, r, value.astype(jnp.bfloat16))

        for r in range(n_rows):
            first_row(r)
        send(*field(t + 1, 0))
        arrived(field(t, 1))

        def second_row(r, t=t):
            value = coef_h[r] * product(t, 1, r) + coef_l[r] * labels[r, :, half:]
            value = value.astype(jnp.bfloat16)
            keep(t + 1, 1, r, value)
            if t + 1 < ITERS - 1:
                both = value.astype(jnp.float32) + own[(t + 1) * HALVES][r].astype(jnp.float32)
                keep_sum(t + 1, r, jnp.sum(both, axis=1, keepdims=True))

        for r in range(n_rows):
            second_row(r)
        if t + 1 < ITERS - 1:
            send(*sums(t + 1))
        send(*field(t + 1, 1))

    last = ITERS - 1

    def update(h, r):
        return 0.9 * scale[r] * product(last, h, r) + 0.1 * labels[r, :, h * half:(h + 1) * half]

    arrived(field(last, 0))

    def last_first(r):
        coef_h[r] = update(0, r)

    for r in range(n_rows):
        last_first(r)
    arrived(field(last, 1))

    def last_second(r):
        second = update(1, r)
        first = coef_h[r]
        mean = jnp.sum(first + second, axis=1, keepdims=True) * (1.0 / classes)
        inverse = jnp.broadcast_to(1.0 / mean, (bsize, half))
        rows = pl.ds(r * bsize, bsize)
        out_ref[0, rows, :half] = first * inverse
        out_ref[0, rows, half:] = second * inverse

    for r in range(n_rows):
        last_second(r)
    for t in range(ITERS):
        if t < ITERS - 1:
            wait_sent(*sums(t))
        for h in range(HALVES):
            wait_sent(*field(t, h))


def solution(mesh):
    n_grp, n_blk = mesh.shape["grp"], mesh.shape["blk"]

    def on_device(labels, tiles, tile_cols, tile_count, send_blocks):
        n_rows, kmax, bsize = tiles.shape[1:4]
        classes = labels.shape[2]
        half = classes // HALVES
        names = n_rows + 2 * HB + n_grp + 1
        count = ITERS * HALVES
        whole = pltpu.VMEM((n_rows, bsize, half), jnp.float32)
        return pl.pallas_call(
            functools.partial(kernel, n_grp, n_blk),
            name="spreading",
            out_shape=pltpu.VMEM(labels.shape, jnp.float32),
            in_specs=[pl.BlockSpec(memory_space=pl.ANY)] * 5,
            out_specs=pl.BlockSpec(memory_space=pltpu.VMEM),
            scratch_shapes=[pltpu.VMEM((names, bsize, half), jnp.bfloat16)] * count
            + [pltpu.VMEM((n_rows, bsize, half), jnp.bfloat16)] * count
            + [pltpu.VMEM((n_grp - 1, bsize, half), jnp.bfloat16)] * count
            + [pltpu.VMEM((names, 1, bsize), jnp.float32)] * (ITERS - 1)
            + [pltpu.VMEM((n_rows, 1, bsize), jnp.float32)] * (ITERS - 1)
            + [pltpu.VMEM((n_grp - 1, 1, bsize), jnp.float32)] * (ITERS - 1)
            + [
                pltpu.VMEM((n_rows, kmax, bsize, bsize), jnp.bfloat16),
                pltpu.VMEM((n_rows, bsize, classes), jnp.float32),
                whole,
                whole,
                whole,
                whole,
                pltpu.SMEM((1, n_rows, kmax), jnp.int32),
                pltpu.SMEM((1, n_rows), jnp.int32),
                pltpu.SMEM((1, 1, n_grp), jnp.int32),
                pltpu.SMEM((n_rows, kmax), jnp.int32),
                pltpu.SemaphoreType.DMA((2 * n_rows,)),
                pltpu.SemaphoreType.DMA((3,)),
                pltpu.SemaphoreType.DMA((count, 3)),
                pltpu.SemaphoreType.DMA((count, 3)),
                pltpu.SemaphoreType.DMA((ITERS - 1, 3)),
                pltpu.SemaphoreType.DMA((ITERS - 1, 3)),
            ],
            compiler_params=pltpu.CompilerParams(
                collective_id=0, has_side_effects=True, vmem_limit_bytes=32 << 20
            ),
        )(*(
            pltpu.with_memory_space_constraint(a, pltpu.HBM)
            for a in (tile_cols, tile_count, send_blocks.reshape(1, 1, n_grp), labels, tiles)
        ))

    return jax.shard_map(
        on_device,
        mesh=mesh,
        in_specs=(
            P("grp", "blk", None),
            P("grp", "blk", None, None, None),
            P("grp", "blk", None),
            P("grp", "blk"),
            P("grp", "blk", None, None),
        ),
        out_specs=P("grp", "blk", None),
        check_vma=False,
    )
```

```python
import functools

import jax
import jax.numpy as jnp
from jax import lax
from jax.experimental import pallas as pl
from jax.experimental.pallas import tpu as pltpu
from jax.sharding import PartitionSpec as P

HB = 2
ITERS = 3
HALVES = 2
PIECE = 64
ORDER = (
    (2, 2), (0, 1), (1, 2), (3, 0), (2, 1), (0, 3), (3, 2), (1, 0), (2, 3), (1, 1), (3, 3), (0, 2), (1, 3), (3, 1), (2, 0),
)
MESH = pl.DeviceIdType.MESH


def kernel(n_grp, n_blk, cols_hbm, count_hbm, pick_hbm, labels_hbm, tiles_hbm, out_ref, *scratch):
    ext = scratch[0:6]
    own = scratch[6:12]
    staged = scratch[12:18]
    ext_sum = scratch[18:20]
    own_sum = scratch[20:22]
    staged_sum = scratch[22:24]
    (tiles, labels, scale, anchor_sum, coef_h, coef_l, cols_ref, count_ref, pick_ref, col, load_sem, small_sem, send_sem, recv_sem,
     send_sum, recv_sum) = scratch[24:]
    n_rows, kmax, bsize = tiles.shape[0], tiles.shape[1], tiles.shape[2]
    classes = labels.shape[2]
    half = classes // HALVES
    local = n_rows + 2 * HB
    zero = local + n_grp
    me = lax.axis_index("grp")
    place = lax.axis_index("blk")
    after = lax.rem(place + 1, n_blk)
    before = lax.rem(place + n_blk - 1, n_blk)

    def load(r):
        return (
            pltpu.make_async_copy(tiles_hbm.at[0, r], tiles.at[r], load_sem.at[r]),
            pltpu.make_async_copy(labels_hbm.at[0, pl.ds(r * bsize, bsize)], labels.at[r], load_sem.at[n_rows + r]),
        )

    if n_grp == 16:
        y, x = lax.div(me, 4), lax.rem(me, 4)
        others = [lax.rem(y + dy, 4) * 4 + lax.rem(x + dx, 4) for dy, dx in ORDER]
    else:
        others = [lax.rem(me + p, n_grp) for p in range(1, n_grp)]

    barrier = pltpu.get_barrier_semaphore()
    for other in others:
        pl.semaphore_signal(barrier, inc=1, device_id={"grp": other}, device_id_type=MESH)
    pl.semaphore_signal(barrier, inc=1, device_id={"blk": after}, device_id_type=MESH)
    pl.semaphore_signal(barrier, inc=1, device_id={"blk": before}, device_id_type=MESH)

    small = [
        pltpu.make_async_copy(src, dst, small_sem.at[i])
        for i, (src, dst) in enumerate(((cols_hbm, cols_ref), (count_hbm, count_ref), (pick_hbm, pick_ref)))
    ]
    for copy in small:
        copy.start()
    for r in range(n_rows):
        for copy in load(r):
            copy.start()

    def name_row(r, carry):
        used = count_ref[0, r]
        for k in range(kmax):
            c = cols_ref[0, r, k]
            block = place * n_rows + c - HB
            outside = (c < local) & ((block < 0) | (block >= n_blk * n_rows))
            col[r, k] = jnp.where((k < used) & jnp.logical_not(outside), c, zero)
        return carry

    for copy in small:
        copy.wait()
    lax.fori_loop(0, n_rows, name_row, 0)
    for ref in ext:
        ref[zero] = jnp.zeros((bsize, half), jnp.bfloat16)
    for ref in ext_sum:
        ref[zero] = jnp.zeros((1, bsize), jnp.float32)

    def keep(t, h, r, value):
        own[t * HALVES + h][r] = value
        ext[t * HALVES + h][HB + r] = value

    def keep_sum(t, r, total):
        at_row = lax.broadcasted_iota(jnp.int32, (bsize, bsize), 0)
        at_col = lax.broadcasted_iota(jnp.int32, (bsize, bsize), 1)
        spread = jnp.where(at_row == at_col, jnp.broadcast_to(total, (bsize, bsize)), 0.0)
        row = jnp.sum(spread, axis=0, keepdims=True)
        own_sum[t][r] = row
        ext_sum[t][HB + r] = row

    def halo_copies(mine, theirs, ssem, rsem, t):
        return (
            pltpu.make_async_remote_copy(
                src_ref=mine.at[pl.ds(n_rows - HB, HB)], dst_ref=theirs.at[pl.ds(0, HB)],
                send_sem=ssem.at[t, 1], recv_sem=rsem.at[t, 1], device_id={"blk": after}, device_id_type=MESH,
            ),
            pltpu.make_async_remote_copy(
                src_ref=mine.at[pl.ds(0, HB)], dst_ref=theirs.at[pl.ds(HB + n_rows, HB)],
                send_sem=ssem.at[t, 2], recv_sem=rsem.at[t, 2], device_id={"blk": before}, device_id_type=MESH,
            ),
        )

    def pick(mine, out):
        for i, other in enumerate(others):
            out[i] = mine[pick_ref[0, 0, other]]

    def send(mine, out, theirs, ssem, rsem, t, picked=False):
        height = mine.shape[1]
        piece = min(PIECE, height)
        for first in range(0, height, piece):
            rows = pl.ds(first, piece)
            for i, other in enumerate(others):
                if first == 0 and not picked:
                    out[i] = mine[pick_ref[0, 0, other]]
                pltpu.make_async_remote_copy(
                    src_ref=out.at[i, rows], dst_ref=theirs.at[local + me, rows],
                    send_sem=ssem.at[t, 0], recv_sem=rsem.at[t, 0], device_id={"grp": other}, device_id_type=MESH,
                ).start()
        for copy in halo_copies(mine, theirs, ssem, rsem, t):
            copy.start()
        theirs[local + me] = mine[pick_ref[0, 0, me]]

    def wait_sent(mine, out, theirs, ssem, rsem, t):
        whole = out.at[pl.ds(0, n_grp - 1)]
        pltpu.make_async_copy(whole, whole, ssem.at[t, 0]).wait()
        for copy in halo_copies(mine, theirs, ssem, rsem, t):
            copy.wait_send()

    def wait_here(mine, theirs, ssem, rsem, t):
        whole = theirs.at[pl.ds(local, n_grp - 1)]
        pltpu.make_async_copy(whole, whole, rsem.at[t, 0]).wait()
        for copy in halo_copies(mine, theirs, ssem, rsem, t):
            copy.wait_recv()

    def field(t, h):
        i = t * HALVES + h
        return own[i], staged[i], ext[i], send_sem, recv_sem, i

    def sums(t):
        return own_sum[t], staged_sum[t], ext_sum[t], send_sum, recv_sum, t

    def arrived(of):
        wait_here(of[0], of[2], *of[3:])

    def product(t, h, r):
        blocks = ext[t * HALVES + h]
        lhs = jnp.concatenate([tiles[r, k] for k in range(kmax)], axis=1)
        rhs = jnp.concatenate([blocks[col[r, k]] for k in range(kmax)], axis=0)
        return jnp.dot(lhs, rhs, preferred_element_type=jnp.float32)

    for r in range(n_rows):
        for copy in load(r):
            copy.wait()
        total = jnp.zeros((bsize, bsize), jnp.float32)
        used = count_ref[0, r]
        for k in range(kmax // 2):
            total += tiles[r, k].astype(jnp.float32) * jnp.where(k < used, 1.0, 0.0)
        later = range(kmax // 2, kmax)
        ones = [jnp.broadcast_to(jnp.where(k < used, 1.0, 0.0), (bsize, half)).astype(jnp.bfloat16) for k in later]
        deg = jnp.sum(total, axis=1, keepdims=True) + jnp.dot(
            jnp.concatenate([tiles[r, k] for k in later], axis=1),
            jnp.concatenate(ones, axis=0),
            preferred_element_type=jnp.float32,
        )
        factor = lax.rsqrt(deg)
        scale[r] = factor
        keep(0, 0, r, (factor * labels[r, :, :half]).astype(jnp.bfloat16))
    pick(*field(0, 0)[:2])
    pl.semaphore_wait(barrier, n_grp + 1)
    send(*field(0, 0), picked=True)
    for r in range(n_rows):
        value = (scale[r] * labels[r, :, half:]).astype(jnp.bfloat16)
        keep(0, 1, r, value)
        both = value.astype(jnp.float32) + own[0][r].astype(jnp.float32)
        keep_sum(0, r, jnp.sum(both, axis=1, keepdims=True))
    send(*sums(0))
    send(*field(0, 1))

    def anchor_row(r):
        total = jnp.sum(labels[r, :, :half] + labels[r, :, half:], axis=1, keepdims=True)
        anchor_sum[r] = jnp.broadcast_to(total, (bsize, half))

    for r in range(n_rows):
        anchor_row(r)

    for t in range(ITERS - 1):
        arrived(sums(t))
        arrived(field(t, 0))

        def first_row(r, t=t):
            h_first = product(t, 0, r)
            total = jnp.zeros((bsize, bsize), jnp.float32)
            for k in range(kmax):
                total += tiles[r, k].astype(jnp.float32) * ext_sum[t][col[r, k]]
            total = jnp.broadcast_to(jnp.sum(total, axis=1, keepdims=True), (bsize, half))
            factor = scale[r]
            mean = (0.9 * factor * total + 0.1 * anchor_sum[r]) * (1.0 / classes)
            inverse = factor / mean
            for_h = 0.9 * factor * inverse
            for_l = 0.1 * inverse
            coef_h[r] = for_h
            coef_l[r] = for_l
            value = for_h * h_first + for_l * labels[r, :, :half]
            keep(t + 1, 0, r, value.astype(jnp.bfloat16))

        for r in range(n_rows):
            first_row(r)
        send(*field(t + 1, 0))
        arrived(field(t, 1))

        def second_row(r, t=t):
            value = coef_h[r] * product(t, 1, r) + coef_l[r] * labels[r, :, half:]
            value = value.astype(jnp.bfloat16)
            keep(t + 1, 1, r, value)
            if t + 1 < ITERS - 1:
                both = value.astype(jnp.float32) + own[(t + 1) * HALVES][r].astype(jnp.float32)
                keep_sum(t + 1, r, jnp.sum(both, axis=1, keepdims=True))

        for r in range(n_rows):
            second_row(r)
        if t + 1 < ITERS - 1:
            send(*sums(t + 1))
        send(*field(t + 1, 1))

    last = ITERS - 1

    def update(h, r):
        return 0.9 * scale[r] * product(last, h, r) + 0.1 * labels[r, :, h * half:(h + 1) * half]

    arrived(field(last, 0))

    def last_first(r):
        coef_h[r] = update(0, r)

    for r in range(n_rows):
        last_first(r)
    arrived(field(last, 1))

    def last_second(r):
        second = update(1, r)
        first = coef_h[r]
        mean = jnp.sum(first + second, axis=1, keepdims=True) * (1.0 / classes)
        inverse = jnp.broadcast_to(1.0 / mean, (bsize, half))
        rows = pl.ds(r * bsize, bsize)
        out_ref[0, rows, :half] = first * inverse
        out_ref[0, rows, half:] = second * inverse

    for r in range(n_rows):
        last_second(r)
    for t in range(ITERS):
        if t < ITERS - 1:
            wait_sent(*sums(t))
        for h in range(HALVES):
            wait_sent(*field(t, h))


def solution(mesh):
    n_grp, n_blk = mesh.shape["grp"], mesh.shape["blk"]

    def on_device(labels, tiles, tile_cols, tile_count, send_blocks):
        n_rows, kmax, bsize = tiles.shape[1:4]
        classes = labels.shape[2]
        half = classes // HALVES
        names = n_rows + 2 * HB + n_grp + 1
        count = ITERS * HALVES
        whole = pltpu.VMEM((n_rows, bsize, half), jnp.float32)
        return pl.pallas_call(
            functools.partial(kernel, n_grp, n_blk),
            name="spreading",
            out_shape=pltpu.VMEM(labels.shape, jnp.float32),
            in_specs=[pl.BlockSpec(memory_space=pl.ANY)] * 5,
            out_specs=pl.BlockSpec(memory_space=pltpu.VMEM),
            scratch_shapes=[pltpu.VMEM((names, bsize, half), jnp.bfloat16)] * count
            + [pltpu.VMEM((n_rows, bsize, half), jnp.bfloat16)] * count
            + [pltpu.VMEM((n_grp - 1, bsize, half), jnp.bfloat16)] * count
            + [pltpu.VMEM((names, 1, bsize), jnp.float32)] * (ITERS - 1)
            + [pltpu.VMEM((n_rows, 1, bsize), jnp.float32)] * (ITERS - 1)
            + [pltpu.VMEM((n_grp - 1, 1, bsize), jnp.float32)] * (ITERS - 1)
            + [
                pltpu.VMEM((n_rows, kmax, bsize, bsize), jnp.bfloat16),
                pltpu.VMEM((n_rows, bsize, classes), jnp.float32),
                whole,
                whole,
                whole,
                whole,
                pltpu.SMEM((1, n_rows, kmax), jnp.int32),
                pltpu.SMEM((1, n_rows), jnp.int32),
                pltpu.SMEM((1, 1, n_grp), jnp.int32),
                pltpu.SMEM((n_rows, kmax), jnp.int32),
                pltpu.SemaphoreType.DMA((2 * n_rows,)),
                pltpu.SemaphoreType.DMA((3,)),
                pltpu.SemaphoreType.DMA((count, 3)),
                pltpu.SemaphoreType.DMA((count, 3)),
                pltpu.SemaphoreType.DMA((ITERS - 1, 3)),
                pltpu.SemaphoreType.DMA((ITERS - 1, 3)),
            ],
            compiler_params=pltpu.CompilerParams(
                collective_id=0, has_side_effects=True, vmem_limit_bytes=32 << 20
            ),
        )(*(
            pltpu.with_memory_space_constraint(a, pltpu.HBM)
            for a in (tile_cols, tile_count, send_blocks.reshape(1, 1, n_grp), labels, tiles)
        ))

    return jax.shard_map(
        on_device,
        mesh=mesh,
        in_specs=(
            P("grp", "blk", None),
            P("grp", "blk", None, None, None),
            P("grp", "blk", None),
            P("grp", "blk"),
            P("grp", "blk", None, None),
        ),
        out_specs=P("grp", "blk", None),
        check_vma=False,
    )
```
